32 devices in a mesh: groups: 2 (over x), dp: 16 (over z, y, core).
Axes of the slice: x: 2, y: 2, z: 4, core: 2. Of those that a mesh axis runs over, the one named last changes fastest.
Arguments:
- patches: bfloat16 [16384, 1280], P(('groups', 'dp')), parts along dimension 0, may hold values from -8 to 8
- send_index: int32 [32, 16, 32], P(('groups', 'dp')), parts along dimension 0, may hold values from -1 to 511, as said below
- window_id: int32 [16384], P(('groups', 'dp')), parts along dimension 0, may hold values from -1 to 8, as said below
- norm_gain: float32 [1280], replicated, may hold values from 0.5 to 5
- w_qkv: bfloat16 [1280, 1920], replicated, may hold values from -0.15625 to 0.15625
- w_proj: bfloat16 [640, 1280], replicated, may hold values from -0.25 to 0.25
- out_grad: bfloat16 [16384, 1280], P(('groups', 'dp')), parts along dimension 0, may hold values from -6 to 6
Outputs:
- embeds: bfloat16 [16384, 1280], P(('groups', 'dp')), parts along dimension 0
- patch_grad: bfloat16 [16384, 1280], P(('groups', 'dp')), parts along dimension 0
- qkv_grad: float32 [2560, 1920], P(('groups', 'dp')), parts along dimension 0
- proj_grad: float32 [1280, 1280], P('groups', 'dp'), parts along dimension 0
The draws below stay inside these ranges and needn't reach their ends.
There are 2 independent parts, one for each index of `groups`. The reference program is written for one: setup_inputs(seed, part) draws one part's arguments, and reference() takes and returns one part's arrays. A program takes and returns all parts, laid end to end along the dimension named above; an argument that names none is the same for every part. Nothing has to cross between parts.
Inputs may be any that keep to these rules, and one draw needn't show every extreme that they name: send_index[s, d, c] is the row of device s that fills slot c of device d, -1 for an empty slot. The filled slots of each pair come first; the rows below the number of filled slots of device s are each sent exactly once and the rows above are sent nowhere. Some device receives 32 rows from every device and some device sends 32 rows to every device. window_id is -1 exactly on empty received slots; the windows of a device are numbered from 0 without gaps and hold at most 64 slots each, spread over the device's slots.
All inputs are finite; a program needn't handle non-finite values.
Results may differ from the reference program's by a relative error of at most 0.0055.
The reference program's roundings to bfloat16 on the way count: a program that leaves them out, or rounds other values in their place, can miss the bound.
Values may be sent and summed in bfloat16 or wider, within the bound.
A program may use at most 128 MiB of HBM per device.

```python
import math
import jax
import jax.numpy as jnp
from jax import lax

D = 1280
HEADS = 8
HDIM = 80
WIN = 64
SLOTS = 512
CAP = 32
TOKENS = 8192
INNER = 640
QKV = 1920
N_DP = 16


def routing_tables(key):
    key = jax.random.fold_in(key, 11)
    keys = jax.random.split(key, 7)
    ranks_count = N_DP
    heavy = jax.random.randint(keys[0], (ranks_count,), CAP // 2, 2 * CAP + 1)
    counts = jax.random.randint(keys[1], (ranks_count, ranks_count), 0, 1 << 20) % (heavy[None, :] + 1)
    counts = jnp.minimum(counts, CAP)
    full_dest = jax.random.randint(keys[2], (), 0, ranks_count)
    full_source = jax.random.randint(keys[3], (), 0, ranks_count)
    lanes = jnp.arange(ranks_count)
    counts = jnp.where(lanes[:, None] == full_dest, CAP, counts)
    counts = jnp.where(lanes[None, :] == full_source, CAP, counts)
    slot_live = jnp.arange(CAP)[None, None, :] < counts[:, :, None]
    source_live = jnp.transpose(slot_live, (1, 0, 2)).reshape(ranks_count, SLOTS)
    order_keys = jax.random.split(keys[4], ranks_count)
    priority = jax.vmap(lambda k: jax.random.permutation(k, SLOTS))(order_keys)
    ordered = jnp.argsort(jnp.where(source_live, priority, SLOTS + priority), axis=1)
    rank = jnp.argsort(ordered, axis=1)
    send = jnp.where(source_live, rank, -1).reshape(ranks_count, ranks_count, CAP)
    dest_live = slot_live.reshape(ranks_count, SLOTS)
    dest_keys = jax.random.split(keys[5], ranks_count)
    dest_priority = jax.vmap(lambda k: jax.random.permutation(k, SLOTS))(dest_keys)
    dest_order = jnp.argsort(jnp.where(dest_live, dest_priority, SLOTS + dest_priority), axis=1)
    dest_rank = jnp.argsort(dest_order, axis=1)
    offset = jax.random.randint(keys[6], (ranks_count,), 0, WIN)
    offset = jnp.where(lanes == full_dest, WIN - 1, offset)
    windows = jnp.where(dest_live, (dest_rank + offset[:, None]) // WIN, -1)
    return (send.astype(jnp.int32), windows.reshape(-1).astype(jnp.int32))


def draw_send_index(key, part):
    return routing_tables(key)[0]


def draw_window_id(key, part):
    return routing_tables(key)[1]


def draw_patches(key, part):
    key = jax.random.fold_in(key, 5)
    first, second = jax.random.split(key)
    row_scale = jnp.exp(jax.random.uniform(second, (TOKENS, 1), jnp.float32, math.log(0.3), math.log(3.0)))
    base = jnp.clip(jax.random.normal(first, (TOKENS, D), jnp.float32), -2.5, 2.5)
    return (base * row_scale).astype(jnp.bfloat16)


def draw_norm_gain(key, part):
    key = jax.random.fold_in(key, 7)
    gains = jax.random.uniform(key, (D,), jnp.float32, 0.5, 1.5)
    return gains


def raised(result, own_key, source, target, shards_of, factor):
    owner, partner = [(jnp.arange(result.shape[dim]) // (result.shape[dim] // shards_of)).reshape([-1 if axis == dim else 1 for axis in range(result.ndim)]) for dim in (source, target)]
    chosen = jax.random.permutation(own_key, shards_of)[partner]
    strong = (owner == chosen) | (owner == (partner + shards_of // 2) % shards_of)
    return jnp.where(strong, factor * result, result)


def shard_levels(own_key, shape, pieces, least, high):
    level = 1.0
    for position, shards_of in pieces:
        heights = jax.random.uniform(jax.random.fold_in(jax.random.fold_in(own_key, 6), position), (shards_of,), jnp.float32, least / len(pieces), high / len(pieces))
        level = level * jnp.repeat(jnp.exp(heights), shape[position] // shards_of).reshape((-1,) + (1,) * (len(shape) - 1 - position))
    return level


def scatter_about(key, extent, deviation, reach, cuts=(), held_as=jnp.bfloat16):
    entries = jax.random.normal(key, extent, jnp.float32) * deviation
    if len(cuts) > 0:
        entries = shard_levels(key, extent, cuts, -0.22, 0.18) * entries
    return jnp.clip(entries, min=-reach, max=reach).astype(held_as)


def gaussian_with(own_key, dims, deviation, bound, cuts, heavy, held_as=jnp.bfloat16):
    drawn = deviation * jax.random.normal(own_key, dims, jnp.float32)
    if cuts:
        drawn = drawn * shard_levels(own_key, dims, cuts, -0.22, 0.18)
    return jnp.clip(raised(drawn, jax.random.fold_in(own_key, 3), *heavy), -bound, bound).astype(held_as)


def setup_inputs(seed: int = 0, part: int = 0) -> dict:
    splits = jax.random.split(jax.random.key(seed), 8)
    own_keys = jax.random.split(jax.random.fold_in(splits[7], part), 8)
    patches = draw_patches(jax.random.fold_in(jax.random.fold_in(splits[7], part), 71), part)
    send_index = draw_send_index(jax.random.fold_in(jax.random.fold_in(splits[7], part), 71), part)
    window_id = draw_window_id(jax.random.fold_in(jax.random.fold_in(splits[7], part), 71), part)
    norm_gain = draw_norm_gain(jax.random.fold_in(splits[7], 71), part)
    w_qkv = scatter_about(splits[4], (D, QKV), D ** -0.5, 0.15625)
    w_proj = scatter_about(splits[5], (INNER, D), INNER ** -0.5, 0.25)
    out_grad = gaussian_with(own_keys[6], (TOKENS, D), 1.0, 6.0, ((0, 16),), (0, 1, 16, 2.0))
    return {"patches": patches, "send_index": send_index, "window_id": window_id, "norm_gain": norm_gain, "w_qkv": w_qkv, "w_proj": w_proj, "out_grad": out_grad}


def device_block(xrows, grows, windows, norm_gain, w_qkv, w_proj):
    score_scale = 1.0 / math.sqrt(HDIM)
    row_vals = xrows.astype(jnp.float32)
    inv_rms = 1.0 / jnp.sqrt(lax.optimization_barrier(jnp.mean(row_vals * row_vals, axis=-1, keepdims=True)) + 1e-06)
    unit = row_vals * inv_rms
    normed = (unit * norm_gain).astype(jnp.bfloat16)
    qkv = jnp.dot(normed.astype(jnp.float32), w_qkv.astype(jnp.float32)).astype(jnp.bfloat16)
    qkv = qkv.reshape(SLOTS, 3, HEADS, HDIM).astype(jnp.float32)
    queries, keys, values = (qkv[:, 0], qkv[:, 1], qkv[:, 2])
    same_window = windows[:, None] == windows[None, :]
    scores = jnp.einsum('qhd,khd->hqk', queries, keys) * score_scale
    scores = jnp.where(same_window[None], scores, -1e+30)
    top = lax.optimization_barrier(jnp.max(scores, axis=-1, keepdims=True))
    expo = jnp.exp(scores - top)
    probs = expo / lax.optimization_barrier(jnp.sum(expo, axis=-1, keepdims=True))
    probs_low = lax.optimization_barrier(probs.astype(jnp.bfloat16)).astype(jnp.float32)
    attended = jnp.einsum('hqk,khd->qhd', probs_low, values).astype(jnp.bfloat16).reshape(SLOTS, INNER)
    mixed = (row_vals + jnp.dot(attended.astype(jnp.float32), w_proj.astype(jnp.float32))).astype(jnp.bfloat16)
    grad_f32 = grows.astype(jnp.float32)
    d_att = jnp.dot(grad_f32, w_proj.astype(jnp.float32).T).astype(jnp.bfloat16)
    d_att = d_att.astype(jnp.float32).reshape(SLOTS, HEADS, HDIM)
    d_probs = jnp.einsum('qhd,khd->hqk', d_att, values)
    d_scores = probs * (d_probs - lax.optimization_barrier(jnp.sum(probs * d_probs, axis=-1, keepdims=True))) * score_scale
    d_scores = lax.optimization_barrier(d_scores.astype(jnp.bfloat16)).astype(jnp.float32)
    d_query = jnp.einsum('hqk,khd->qhd', d_scores, keys)
    d_key = jnp.einsum('hqk,qhd->khd', d_scores, queries)
    d_value = jnp.einsum('hqk,qhd->khd', probs_low, d_att)
    d_qkv = jnp.stack([d_query, d_key, d_value], axis=1).astype(jnp.bfloat16).reshape(SLOTS, QKV)
    d_normed = jnp.dot(d_qkv.astype(jnp.float32), w_qkv.astype(jnp.float32).T)
    scaled = d_normed * norm_gain
    d_rows = grad_f32 + inv_rms * (scaled - unit * lax.optimization_barrier(jnp.mean(scaled * unit, axis=-1, keepdims=True)))
    return (mixed, d_rows.astype(jnp.bfloat16), attended, d_qkv, normed)

def reference(patches, send_index, window_id, norm_gain, w_qkv, w_proj, out_grad):
    per_dest = jnp.transpose(send_index, (1, 0, 2))
    slot_live = per_dest >= 0
    source_row = jnp.arange(N_DP, dtype=jnp.int32)[None, :, None] * SLOTS + per_dest
    pick = jnp.where(slot_live, source_row, 0).reshape(-1).astype(jnp.int32)
    live_flat = slot_live.reshape(-1)[:, None]
    gathered = jnp.where(live_flat, patches[pick], jnp.zeros((), jnp.bfloat16))
    grad_in = jnp.where(live_flat, out_grad[pick], jnp.zeros((), jnp.bfloat16))

    def one_device(items):
        return device_block(items[0], items[1], items[2], norm_gain, w_qkv, w_proj)
    mixed, d_rows, attended, d_qkv, normed = lax.map(one_device, (gathered.reshape(N_DP, SLOTS, D), grad_in.reshape(N_DP, SLOTS, D), window_id.reshape(N_DP, SLOTS)))
    target = jnp.where(slot_live, source_row, TOKENS).reshape(-1).astype(jnp.int32)
    embeds = jnp.zeros((TOKENS, D), jnp.bfloat16).at[target].set(mixed.reshape(TOKENS, D), mode='drop')
    patch_grad = jnp.zeros((TOKENS, D), jnp.bfloat16).at[target].set(d_rows.reshape(TOKENS, D), mode='drop')
    grad_scale = 1.0 / math.sqrt(TOKENS)
    proj_grad = jnp.dot(attended.reshape(TOKENS, INNER).astype(jnp.float32).T, grad_in.astype(jnp.float32)) * grad_scale
    qkv_grad = jnp.dot(normed.reshape(TOKENS, D).astype(jnp.float32).T, d_qkv.reshape(TOKENS, QKV).astype(jnp.float32)) * grad_scale
    return (embeds, patch_grad, qkv_grad, proj_grad)
```

```python
import functools
import math

import jax
import jax.numpy as jnp
from jax import lax
from jax.experimental import pallas as pl
from jax.experimental.pallas import tpu as pltpu
from jax.sharding import PartitionSpec as P

HEADS = 8
HDIM = 80


def contract_rows(left, right):
    return lax.dot_general(
        left, right, (((0,), (0,)), ((), ())), preferred_element_type=jnp.float32
    )


def contract_cols(left, right):
    return lax.dot_general(
        left, right, (((1,), (1,)), ((), ())), preferred_element_type=jnp.float32
    )


def shards(patches, send_index, window_id, norm_gain, w_qkv, w_proj, out_grad):
    peer_count = lax.axis_size("dp")
    slot_count = patches.shape[0]
    per_peer = send_index.shape[2]
    width = patches.shape[1]
    heads = HEADS
    head_size = HDIM
    inner_width = heads * head_size
    qkv_width = 3 * inner_width
    score_scale = 1.0 / math.sqrt(head_size)
    grad_scale = 1.0 / math.sqrt(slot_count * peer_count)
    send_rows = send_index[0]
    slot_live = send_rows >= 0
    safe_rows = jnp.maximum(send_rows, 0).reshape(-1)

    def pack(rows):
        picked = jnp.take(rows, safe_rows, axis=0).reshape(peer_count, per_peer, width)
        return jnp.where(slot_live[:, :, None], picked, jnp.zeros((), rows.dtype))

    def unpack(rows):
        target = jnp.where(slot_live, send_rows, slot_count).reshape(-1)
        flat_rows = rows.reshape(peer_count * per_peer, width)
        return jnp.zeros((slot_count, width), jnp.bfloat16).at[target].set(flat_rows, mode="drop")

    sent_rows, sent_grads = (
        lax.all_to_all(pack(patches), "dp", split_axis=0, concat_axis=0, tiled=True),
        lax.all_to_all(pack(out_grad), "dp", split_axis=0, concat_axis=0, tiled=True),
    )
    gathered = sent_rows.reshape(slot_count, width)
    grad_in = sent_grads.reshape(slot_count, width)
    row_vals = gathered.astype(jnp.float32)
    inv_rms = lax.rsqrt(jnp.mean(row_vals * row_vals, axis=-1, keepdims=True) + 1e-06)
    unit = row_vals * inv_rms
    normed = (unit * norm_gain).astype(jnp.bfloat16)
    qkv = jnp.dot(normed, w_qkv, preferred_element_type=jnp.float32).astype(jnp.bfloat16)
    qkv = qkv.reshape(slot_count, 3, heads, head_size)
    queries, keys, values = (qkv[:, 0], qkv[:, 1], qkv[:, 2])
    same_window = window_id[:, None] == window_id[None, :]
    scores = (
        jnp.einsum("qhd,khd->hqk", queries, keys, preferred_element_type=jnp.float32) * score_scale
    )
    scores = jnp.where(same_window[None], scores, -1e30)
    top = jnp.max(scores, axis=-1, keepdims=True)
    expo = jnp.exp(scores - top)
    probs = expo / jnp.sum(expo, axis=-1, keepdims=True)
    probs_low = probs.astype(jnp.bfloat16)
    attended = jnp.einsum("hqk,khd->qhd", probs_low, values, preferred_element_type=jnp.float32)
    attended = attended.astype(jnp.bfloat16).reshape(slot_count, inner_width)
    mixed = (row_vals + jnp.dot(attended, w_proj, preferred_element_type=jnp.float32)).astype(
        jnp.bfloat16
    )
    proj_term = contract_rows(attended, grad_in) * grad_scale
    d_att = (
        contract_cols(grad_in, w_proj).astype(jnp.bfloat16).reshape(slot_count, heads, head_size)
    )
    d_probs = jnp.einsum("qhd,khd->hqk", d_att, values, preferred_element_type=jnp.float32)
    d_scores = probs * (d_probs - jnp.sum(probs * d_probs, axis=-1, keepdims=True)) * score_scale
    d_scores = d_scores.astype(jnp.bfloat16)
    d_query = jnp.einsum("hqk,khd->qhd", d_scores, keys, preferred_element_type=jnp.float32)
    d_key = jnp.einsum("hqk,qhd->khd", d_scores, queries, preferred_element_type=jnp.float32)
    d_value = jnp.einsum("hqk,qhd->khd", probs_low, d_att, preferred_element_type=jnp.float32)
    d_qkv = (
        jnp.stack([d_query, d_key, d_value], axis=1)
        .astype(jnp.bfloat16)
        .reshape(slot_count, qkv_width)
    )
    qkv_term = contract_rows(normed, d_qkv) * grad_scale
    qkv_grad, proj_grad = (
        lax.psum_scatter(qkv_term, "dp", scatter_dimension=0, tiled=True),
        lax.psum_scatter(proj_term, "dp", scatter_dimension=1, tiled=True),
    )
    d_normed = contract_cols(d_qkv, w_qkv)
    scaled = d_normed * norm_gain
    d_rows = grad_in.astype(jnp.float32) + inv_rms * (
        scaled - unit * jnp.mean(scaled * unit, axis=-1, keepdims=True)
    )
    d_rows = d_rows.astype(jnp.bfloat16)
    back_out, back_grad = (
        lax.all_to_all(
            mixed.reshape(peer_count, per_peer, width),
            "dp",
            split_axis=0,
            concat_axis=0,
            tiled=True,
        ),
        lax.all_to_all(
            d_rows.reshape(peer_count, per_peer, width),
            "dp",
            split_axis=0,
            concat_axis=0,
            tiled=True,
        ),
    )
    embeds = unpack(back_out)
    patch_grad = unpack(back_grad)
    return (embeds, patch_grad, qkv_grad, proj_grad)


MESH = pl.DeviceIdType.MESH
F32, BF16 = jnp.float32, jnp.bfloat16


def rev(value, bits):
    out = 0
    for _ in range(bits):
        out = out * 2 + value % 2
        value = value // 2
    return out


def mm(left, right):
    return jnp.dot(left, right, preferred_element_type=F32)


def block_kernel(
    n, idx_col, idx_row, wid_col, wid_row, gain, patches, out_grad, w_qkv, w_proj,
    embeds, patch_grad, qkv_out, proj_out,
    packed, landed, back, normed, tall, qkvh, atth, flat, inv, term, inbox,
    a_send, a_recv, r_send, r_recv,
):
    me = lax.axis_index("dp")
    slots, width = patches.shape
    cap = slots // n
    bits = n.bit_length() - 1
    inner = w_proj.shape[0]
    own = width // n
    scale = 1.0 / math.sqrt(HDIM)
    grad_scale = 1.0 / math.sqrt(slots * n)

    barrier = pltpu.get_barrier_semaphore()

    def greet(k, carry):
        pl.semaphore_signal(
            barrier, inc=1, device_id={"dp": lax.rem(me + k, n)}, device_id_type=MESH
        )
        return carry

    lax.fori_loop(1, n, greet, 0)

    def rows_of(p):
        return pl.ds(pl.multiple_of(p * cap, cap), cap)

    def row_copy(src, dst, t, k):
        peer = lax.rem(me + k, n)
        return pltpu.make_async_remote_copy(
            src_ref=src.at[rows_of(peer)],
            dst_ref=dst.at[rows_of(me)],
            send_sem=a_send.at[t, k],
            recv_sem=a_recv.at[t, k],
            device_id={"dp": peer},
            device_id_type=MESH,
        )

    def send_rows(src, dst, t):
        def go(k, carry):
            row_copy(src, dst, t, k).start()
            return carry

        lax.fori_loop(1, n, go, 0)
        dst[rows_of(me), :] = src[rows_of(me), :]

    def recv_rows(src, dst, t):
        def go(k, carry):
            row_copy(src, dst, t, k).wait_recv()
            return carry

        lax.fori_loop(1, n, go, 0)

    def sent_rows(src, dst, t):
        def go(k, carry):
            row_copy(src, dst, t, k).wait_send()
            return carry

        lax.fori_loop(1, n, go, 0)

    def share_copy(c, step):
        half = n >> (step + 1)
        base = 0
        for s in range(step):
            base = base + lax.rem(me // (1 << s), 2) * (n >> (s + 1))
        bit = lax.rem(me // (1 << step), 2)
        peer = me + (1 << step) * (1 - 2 * bit)
        away = base + (1 - bit) * half
        kept = base + bit * half
        copy = pltpu.make_async_remote_copy(
            src_ref=term.at[c, pl.ds(away, half)],
            dst_ref=inbox.at[c, pl.ds(half, half)],
            send_sem=r_send.at[c, step],
            recv_sem=r_recv.at[c, step],
            device_id={"dp": peer},
            device_id_type=MESH,
        )
        return copy, kept, half

    def share_start(c, step):
        share_copy(c, step)[0].start()

    def share_add(c, step):
        copy, kept, half = share_copy(c, step)
        copy.wait_recv()

        def add(i, carry):
            term[c, kept + i] = term[c, kept + i] + inbox[c, half + i]
            return carry

        lax.fori_loop(0, half, add, 0)

    def advance(c, step):
        share_add(c, step)
        if step + 1 < bits:
            share_start(c, step + 1)

    def make_term(c, left, right):
        group = 4
        for g in range(n // group):
            part = mm(left[g * group * own:(g + 1) * group * own, :], right) * grad_scale
            for i in range(group):
                term[c, rev(g * group + i, bits)] = part[i * own:(i + 1) * own, :]

    lanes = lax.broadcasted_iota(jnp.int32, (slots, slots), 1)
    pick = jnp.where(lanes == idx_col[...], 1.0, 0.0).astype(BF16)
    packed[0] = mm(pick, patches[...]).astype(BF16)
    pl.semaphore_wait(barrier, n - 1)
    send_rows(packed.at[0], landed.at[0], 0)
    packed[1] = mm(pick, out_grad[...]).astype(BF16)
    send_rows(packed.at[1], landed.at[1], 1)

    recv_rows(packed.at[0], landed.at[0], 0)
    row_vals = landed[0].astype(F32)
    inv[...] = lax.rsqrt(jnp.mean(row_vals * row_vals, axis=-1, keepdims=True) + 1e-06)
    normed[...] = (row_vals * inv[...] * gain[...]).astype(BF16)
    for kind in range(3):
        part = mm(normed[...], w_qkv[:, kind * inner:(kind + 1) * inner]).astype(BF16)
        for h in range(HEADS):
            qkvh[kind, h] = part[:, h * HDIM:(h + 1) * HDIM]

    def probs_of(h):
        scores = contract_cols(qkvh[0, h], qkvh[1, h]) * scale
        scores = jnp.where(wid_col[...] == wid_row[...], scores, -1e30)
        expo = jnp.exp(scores - jnp.max(scores, axis=-1, keepdims=True))
        return expo * (1.0 / jnp.sum(expo, axis=-1, keepdims=True))

    def forward(h, carry):
        atth[h] = mm(probs_of(h).astype(BF16), qkvh[2, h]).astype(BF16)
        return carry

    lax.fori_loop(0, HEADS, forward, 0)
    for h in range(HEADS):
        flat[0, :, h * HDIM:(h + 1) * HDIM] = atth[h]
    sent_rows(packed.at[0], landed.at[0], 0)
    packed[0] = (landed[0].astype(F32) + mm(flat[0], w_proj[...])).astype(BF16)
    send_rows(packed.at[0], back.at[0], 2)

    recv_rows(packed.at[1], landed.at[1], 1)
    tall[...] = landed[1].T
    make_term(0, tall, flat[0])
    share_start(0, 0)
    tall[...] = normed[...].T
    part = contract_cols(landed[1], w_proj[...]).astype(BF16)
    for h in range(HEADS):
        atth[h] = part[:, h * HDIM:(h + 1) * HDIM]

    def backward(h, carry):
        probs = probs_of(h)
        grad = contract_cols(atth[h], qkvh[2, h])
        dsc = probs * (grad - jnp.sum(probs * grad, axis=-1, keepdims=True)) * scale
        dsc = dsc.astype(BF16)
        d_query = mm(dsc, qkvh[1, h]).astype(BF16)
        d_key = contract_rows(dsc, qkvh[0, h]).astype(BF16)
        d_value = contract_rows(probs.astype(BF16), atth[h]).astype(BF16)
        qkvh[0, h] = d_query
        qkvh[1, h] = d_key
        qkvh[2, h] = d_value
        return carry

    lax.fori_loop(0, HEADS // 2, backward, 0)
    advance(0, 0)
    lax.fori_loop(HEADS // 2, HEADS, backward, 0)
    for kind in range(3):
        for h in range(HEADS):
            flat[kind, :, h * HDIM:(h + 1) * HDIM] = qkvh[kind, h]
        make_term(kind + 1, tall, flat[kind])
        share_start(kind + 1, 0)
    advance(0, 1)
    d_normed = contract_cols(flat[0], w_qkv[:, 0:inner])
    for kind in range(1, 3):
        d_normed = d_normed + contract_cols(
            flat[kind], w_qkv[:, kind * inner:(kind + 1) * inner]
        )
    scaled = d_normed * gain[...]
    unit = landed[0].astype(F32) * inv[...]
    d_rows = landed[1].astype(F32) + inv[...] * (
        scaled - unit * jnp.mean(scaled * unit, axis=-1, keepdims=True)
    )
    sent_rows(packed.at[1], landed.at[1], 1)
    packed[1] = d_rows.astype(BF16)
    send_rows(packed.at[1], back.at[1], 3)

    for kind in range(3):
        advance(kind + 1, 0)
    advance(0, 2)
    rows = lax.broadcasted_iota(jnp.int32, (slots, slots), 0)
    place = jnp.where(rows == idx_row[...], 1.0, 0.0).astype(BF16)
    recv_rows(packed.at[0], back.at[0], 2)
    embeds[...] = mm(place, back[0]).astype(BF16)
    for kind in range(3):
        advance(kind + 1, 1)
    advance(0, 3)
    for step in range(2, bits):
        for kind in range(3):
            advance(kind + 1, step)
    recv_rows(packed.at[1], back.at[1], 3)
    patch_grad[...] = mm(place, back[1]).astype(BF16)
    mine = 0
    for s in range(bits):
        mine = mine + lax.rem(me // (1 << s), 2) * (n >> (s + 1))
    proj_out[...] = term[0, mine]
    for kind in range(3):
        qkv_out[:, kind * inner:(kind + 1) * inner] = term[kind + 1, mine]
    sent_rows(packed.at[0], back.at[0], 2)
    sent_rows(packed.at[1], back.at[1], 3)
    for c in range(4):
        for step in range(bits):
            share_copy(c, step)[0].wait_send()


def block(patches, send_index, window_id, norm_gain, w_qkv, w_proj, out_grad):
    n = lax.axis_size("dp")
    slots, width = patches.shape
    inner = w_proj.shape[0]
    own = width // n
    bits = n.bit_length() - 1
    vmem = pl.BlockSpec(memory_space=pltpu.VMEM)
    rows = send_index.reshape(-1)
    dma = pltpu.SemaphoreType.DMA
    embeds, patch_grad, qkv_grad, proj_grad = pl.pallas_call(
        functools.partial(block_kernel, n),
        out_shape=(
            jax.ShapeDtypeStruct((slots, width), BF16),
            jax.ShapeDtypeStruct((slots, width), BF16),
            jax.ShapeDtypeStruct((own, 3 * inner), F32),
            jax.ShapeDtypeStruct((own, inner), F32),
        ),
        in_specs=[vmem] * 9,
        out_specs=[vmem] * 4,
        scratch_shapes=[
            pltpu.VMEM((2, slots, width), BF16),
            pltpu.VMEM((2, slots, width), BF16),
            pltpu.VMEM((2, slots, width), BF16),
            pltpu.VMEM((slots, width), BF16),
            pltpu.VMEM((width, slots), BF16),
            pltpu.VMEM((3, HEADS, slots, HDIM), BF16),
            pltpu.VMEM((HEADS, slots, HDIM), BF16),
            pltpu.VMEM((3, slots, inner), BF16),
            pltpu.VMEM((slots, 1), F32),
            pltpu.VMEM((4, n, own, inner), F32),
            pltpu.VMEM((4, n, own, inner), F32),
            dma((4, n)),
            dma((4, n)),
            dma((4, bits)),
            dma((4, bits)),
        ],
        compiler_params=pltpu.CompilerParams(
            collective_id=0, has_side_effects=True, vmem_limit_bytes=62 * 1024 * 1024
        ),
    )(
        rows[:, None], rows[None, :], window_id[:, None], window_id[None, :],
        norm_gain[None, :], patches, out_grad, w_qkv, w_proj,
    )
    return embeds, patch_grad, qkv_grad, proj_grad.T


def solution(mesh):
    in_specs = (
        P(("groups", "dp"), None),
        P(("groups", "dp"), None, None),
        P(("groups", "dp")),
        P(),
        P(),
        P(),
        P(("groups", "dp"), None),
    )
    out_specs = (
        P(("groups", "dp"), None),
        P(("groups", "dp"), None),
        P(("groups", "dp"), None),
        P("groups", "dp"),
    )

    n = mesh.shape["dp"]

    def run(patches, send_index, *rest):
        width = patches.shape[1]
        fits = send_index.shape[2] % 16 == 0 and n & (n - 1) == 0 and width % (8 * n) == 0
        return jax.shard_map(
            block if fits else shards,
            mesh=mesh, in_specs=in_specs, out_specs=out_specs, check_vma=False,
        )(patches, send_index, *rest)

    return run
```

```python
import functools
import math

import jax
import jax.numpy as jnp
from jax import lax
from jax.experimental import pallas as pl
from jax.experimental.pallas import tpu as pltpu
from jax.sharding import PartitionSpec as P

HEADS = 8
HDIM = 80


def contract_rows(left, right):
    return lax.dot_general(
        left, right, (((0,), (0,)), ((), ())), preferred_element_type=jnp.float32
    )


def contract_cols(left, right):
    return lax.dot_general(
        left, right, (((1,), (1,)), ((), ())), preferred_element_type=jnp.float32
    )


def shards(patches, send_index, window_id, norm_gain, w_qkv, w_proj, out_grad):
    peer_count = lax.axis_size("dp")
    slot_count = patches.shape[0]
    per_peer = send_index.shape[2]
    width = patches.shape[1]
    heads = HEADS
    head_size = HDIM
    inner_width = heads * head_size
    qkv_width = 3 * inner_width
    score_scale = 1.0 / math.sqrt(head_size)
    grad_scale = 1.0 / math.sqrt(slot_count * peer_count)
    send_rows = send_index[0]
    slot_live = send_rows >= 0
    safe_rows = jnp.maximum(send_rows, 0).reshape(-1)

    def pack(rows):
        picked = jnp.take(rows, safe_rows, axis=0).reshape(peer_count, per_peer, width)
        return jnp.where(slot_live[:, :, None], picked, jnp.zeros((), rows.dtype))

    def unpack(rows):
        target = jnp.where(slot_live, send_rows, slot_count).reshape(-1)
        flat_rows = rows.reshape(peer_count * per_peer, width)
        return jnp.zeros((slot_count, width), jnp.bfloat16).at[target].set(flat_rows, mode="drop")

    sent_rows, sent_grads = (
        lax.all_to_all(pack(patches), "dp", split_axis=0, concat_axis=0, tiled=True),
        lax.all_to_all(pack(out_grad), "dp", split_axis=0, concat_axis=0, tiled=True),
    )
    gathered = sent_rows.reshape(slot_count, width)
    grad_in = sent_grads.reshape(slot_count, width)
    row_vals = gathered.astype(jnp.float32)
    inv_rms = lax.rsqrt(jnp.mean(row_vals * row_vals, axis=-1, keepdims=True) + 1e-06)
    unit = row_vals * inv_rms
    normed = (unit * norm_gain).astype(jnp.bfloat16)
    qkv = jnp.dot(normed, w_qkv, preferred_element_type=jnp.float32).astype(jnp.bfloat16)
    qkv = qkv.reshape(slot_count, 3, heads, head_size)
    queries, keys, values = (qkv[:, 0], qkv[:, 1], qkv[:, 2])
    same_window = window_id[:, None] == window_id[None, :]
    scores = (
        jnp.einsum("qhd,khd->hqk", queries, keys, preferred_element_type=jnp.float32) * score_scale
    )
    scores = jnp.where(same_window[None], scores, -1e30)
    top = jnp.max(scores, axis=-1, keepdims=True)
    expo = jnp.exp(scores - top)
    probs = expo / jnp.sum(expo, axis=-1, keepdims=True)
    probs_low = probs.astype(jnp.bfloat16)
    attended = jnp.einsum("hqk,khd->qhd", probs_low, values, preferred_element_type=jnp.float32)
    attended = attended.astype(jnp.bfloat16).reshape(slot_count, inner_width)
    mixed = (row_vals + jnp.dot(attended, w_proj, preferred_element_type=jnp.float32)).astype(
        jnp.bfloat16
    )
    proj_term = contract_rows(attended, grad_in) * grad_scale
    d_att = (
        contract_cols(grad_in, w_proj).astype(jnp.bfloat16).reshape(slot_count, heads, head_size)
    )
    d_probs = jnp.einsum("qhd,khd->hqk", d_att, values, preferred_element_type=jnp.float32)
    d_scores = probs * (d_probs - jnp.sum(probs * d_probs, axis=-1, keepdims=True)) * score_scale
    d_scores = d_scores.astype(jnp.bfloat16)
    d_query = jnp.einsum("hqk,khd->qhd", d_scores, keys, preferred_element_type=jnp.float32)
    d_key = jnp.einsum("hqk,qhd->khd", d_scores, queries, preferred_element_type=jnp.float32)
    d_value = jnp.einsum("hqk,qhd->khd", probs_low, d_att, preferred_element_type=jnp.float32)
    d_qkv = (
        jnp.stack([d_query, d_key, d_value], axis=1)
        .astype(jnp.bfloat16)
        .reshape(slot_count, qkv_width)
    )
    qkv_term = contract_rows(normed, d_qkv) * grad_scale
    qkv_grad, proj_grad = (
        lax.psum_scatter(qkv_term, "dp", scatter_dimension=0, tiled=True),
        lax.psum_scatter(proj_term, "dp", scatter_dimension=1, tiled=True),
    )
    d_normed = contract_cols(d_qkv, w_qkv)
    scaled = d_normed * norm_gain
    d_rows = grad_in.astype(jnp.float32) + inv_rms * (
        scaled - unit * jnp.mean(scaled * unit, axis=-1, keepdims=True)
    )
    d_rows = d_rows.astype(jnp.bfloat16)
    back_out, back_grad = (
        lax.all_to_all(
            mixed.reshape(peer_count, per_peer, width),
            "dp",
            split_axis=0,
            concat_axis=0,
            tiled=True,
        ),
        lax.all_to_all(
            d_rows.reshape(peer_count, per_peer, width),
            "dp",
            split_axis=0,
            concat_axis=0,
            tiled=True,
        ),
    )
    embeds = unpack(back_out)
    patch_grad = unpack(back_grad)
    return (embeds, patch_grad, qkv_grad, proj_grad)


MESH = pl.DeviceIdType.MESH
F32, BF16 = jnp.float32, jnp.bfloat16


def rev(value, bits):
    out = 0
    for _ in range(bits):
        out = out * 2 + value % 2
        value = value // 2
    return out


def mm(left, right):
    return jnp.dot(left, right, preferred_element_type=F32)


def block_kernel(
    n, send_index, window_id, norm_gain, patches, out_grad, w_qkv, w_proj,
    embeds, patch_grad, qkv_out, proj_out,
    packed, landed, back, att, batt, normed, tall, qkvh, atth, flat, inv, gain, idx_row, wid_row,
    wid_col, term, inbox, outbox, in_scale, out_scale, a_send, a_recv, r_send, r_recv,
):
    me = lax.axis_index("dp")
    slots, width = patches.shape
    cap = slots // n
    bits = n.bit_length() - 1
    inner = w_proj.shape[0]
    own = width // n
    scale = 1.0 / math.sqrt(HDIM)
    grad_scale = 1.0 / math.sqrt(slots * n)

    barrier = pltpu.get_barrier_semaphore()

    def greet(k, carry):
        pl.semaphore_signal(
            barrier, inc=1, device_id={"dp": lax.rem(me + k, n)}, device_id_type=MESH
        )
        return carry

    lax.fori_loop(1, n, greet, 0)

    def rows_of(p):
        return pl.ds(pl.multiple_of(p * cap, cap), cap)

    def row_copy(src, dst, t, k):
        peer = lax.rem(me + k, n)
        return pltpu.make_async_remote_copy(
            src_ref=src.at[rows_of(peer)],
            dst_ref=dst.at[rows_of(me)],
            send_sem=a_send.at[t, k],
            recv_sem=a_recv.at[t, k],
            device_id={"dp": peer},
            device_id_type=MESH,
        )

    def send_rows(src, dst, t):
        def go(k, carry):
            row_copy(src, dst, t, k).start()
            return carry

        lax.fori_loop(1, n, go, 0)
        dst[rows_of(me), :] = src[rows_of(me), :]

    def recv_rows(src, dst, t):
        def go(k, carry):
            row_copy(src, dst, t, k).wait_recv()
            return carry

        lax.fori_loop(1, n, go, 0)

    def sent_rows(src, dst, t):
        def go(k, carry):
            row_copy(src, dst, t, k).wait_send()
            return carry

        lax.fori_loop(1, n, go, 0)

    def share_place(step):
        half = n >> (step + 1)
        base = 0
        for s in range(step):
            base = base + lax.rem(me // (1 << s), 2) * (n >> (s + 1))
        bit = lax.rem(me // (1 << step), 2)
        peer = me + (1 << step) * (1 - 2 * bit)
        return peer, base + (1 - bit) * half, base + bit * half, half

    def share_copies(c, step):
        peer, _, _, half = share_place(step)
        part = pl.ds(half, half)
        return [
            pltpu.make_async_remote_copy(
                src_ref=source.at[c, part],
                dst_ref=target.at[c, part],
                send_sem=r_send.at[c, step, kind],
                recv_sem=r_recv.at[c, step, kind],
                device_id={"dp": peer},
                device_id_type=MESH,
            )
            for kind, (source, target) in enumerate(((outbox, inbox), (out_scale, in_scale)))
        ]

    def share_start(c, step):
        _, away, _, half = share_place(step)

        def code(i, carry):
            value = term[c, away + i]
            most = jnp.max(jnp.abs(value), axis=0, keepdims=True)
            factor = jnp.where(most > 1e-30, 32767.0 / jnp.maximum(most, 1e-30), 0.0)
            outbox[c, half + i] = jnp.round(value * factor).astype(jnp.int32).astype(jnp.int16)
            out_scale[c, half + i] = most * (1.0 / 32767.0)
            return carry

        lax.fori_loop(0, half, code, 0)
        for copy in share_copies(c, step):
            copy.start()

    def share_add(c, step):
        _, _, kept, half = share_place(step)
        for copy in share_copies(c, step):
            copy.wait_recv()

        def add(i, carry):
            value = inbox[c, half + i].astype(jnp.int32).astype(F32)
            term[c, kept + i] = term[c, kept + i] + value * in_scale[c, half + i]
            return carry

        lax.fori_loop(0, half, add, 0)

    def advance(c, step):
        share_add(c, step)
        if step + 1 < bits:
            share_start(c, step + 1)

    def make_term(c, left, right):
        group = 4
        for g in range(n // group):
            part = mm(left[g * group * own:(g + 1) * group * own, :], right) * grad_scale
            for i in range(group):
                term[c, rev(g * group + i, bits)] = part[i * own:(i + 1) * own, :]

    for p in range(n):
        idx_row[0:1, p * cap:(p + 1) * cap] = send_index[0, p:p + 1, :]
    wid_row[...] = window_id[...].reshape(1, slots)
    gain[...] = norm_gain[...].reshape(1, width)
    wid_col[...] = jnp.broadcast_to(wid_row[...], (128, slots)).T[:, 0:1]
    rows = lax.broadcasted_iota(jnp.int32, (slots, slots), 0)
    place = jnp.where(rows == idx_row[...], 1.0, 0.0).astype(BF16)
    packed[0] = contract_rows(place, patches[...]).astype(BF16)
    pl.semaphore_wait(barrier, n - 1)
    send_rows(packed.at[0], landed.at[0], 0)
    packed[1] = contract_rows(place, out_grad[...]).astype(BF16)
    send_rows(packed.at[1], landed.at[1], 1)

    recv_rows(packed.at[0], landed.at[0], 0)
    row_vals = landed[0].astype(F32)
    inv[...] = lax.rsqrt(jnp.mean(row_vals * row_vals, axis=-1, keepdims=True) + 1e-06)
    normed[...] = (row_vals * inv[...] * gain[...]).astype(BF16)
    for kind in range(3):
        part = mm(normed[...], w_qkv[:, kind * inner:(kind + 1) * inner]).astype(BF16)
        for h in range(HEADS):
            qkvh[kind, h] = part[:, h * HDIM:(h + 1) * HDIM]

    def probs_of(h):
        scores = contract_cols(qkvh[0, h], qkvh[1, h]) * scale
        scores = jnp.where(wid_col[...] == wid_row[...], scores, -1e30)
        expo = jnp.exp(scores - jnp.max(scores, axis=-1, keepdims=True))
        return expo * (1.0 / jnp.sum(expo, axis=-1, keepdims=True))

    def forward(h, carry):
        atth[h] = mm(probs_of(h).astype(BF16), qkvh[2, h]).astype(BF16)
        return carry

    lax.fori_loop(0, HEADS, forward, 0)
    for h in range(HEADS):
        att[:, h * HDIM:(h + 1) * HDIM] = atth[h]
    send_rows(att, batt, 2)

    recv_rows(packed.at[1], landed.at[1], 1)
    tall[...] = landed[1].T
    make_term(0, tall, att[...])
    share_start(0, 0)
    tall[...] = normed[...].T
    part = contract_cols(landed[1], w_proj[...]).astype(BF16)
    for h in range(HEADS):
        atth[h] = part[:, h * HDIM:(h + 1) * HDIM]

    def backward(h, carry):
        probs = probs_of(h)
        grad = contract_cols(atth[h], qkvh[2, h])
        dsc = probs * (grad - jnp.sum(probs * grad, axis=-1, keepdims=True)) * scale
        dsc = dsc.astype(BF16)
        d_query = mm(dsc, qkvh[1, h]).astype(BF16)
        d_key = contract_rows(dsc, qkvh[0, h]).astype(BF16)
        d_value = contract_rows(probs.astype(BF16), atth[h]).astype(BF16)
        qkvh[0, h] = d_query
        qkvh[1, h] = d_key
        qkvh[2, h] = d_value
        return carry

    lax.fori_loop(0, HEADS // 2, backward, 0)
    advance(0, 0)
    lax.fori_loop(HEADS // 2, HEADS, backward, 0)
    for kind in range(3):
        for h in range(HEADS):
            flat[kind, :, h * HDIM:(h + 1) * HDIM] = qkvh[kind, h]
        make_term(kind + 1, tall, flat[kind])
        share_start(kind + 1, 0)
    advance(0, 1)
    d_normed = contract_cols(flat[0], w_qkv[:, 0:inner])
    for kind in range(1, 3):
        d_normed = d_normed + contract_cols(
            flat[kind], w_qkv[:, kind * inner:(kind + 1) * inner]
        )
    scaled = d_normed * gain[...]
    unit = landed[0].astype(F32) * inv[...]
    d_rows = landed[1].astype(F32) + inv[...] * (
        scaled - unit * jnp.mean(scaled * unit, axis=-1, keepdims=True)
    )
    sent_rows(packed.at[1], landed.at[1], 1)
    packed[1] = d_rows.astype(BF16)
    send_rows(packed.at[1], back, 3)

    for kind in range(3):
        advance(kind + 1, 0)
    advance(0, 2)
    place = jnp.where(rows == idx_row[...], 1.0, 0.0)
    live = jnp.sum(place, axis=-1, keepdims=True)
    place = place.astype(BF16)
    recv_rows(att, batt, 2)
    home = mm(place, batt[...]).astype(BF16)
    embeds[...] = (patches[...].astype(F32) * live + mm(home, w_proj[...])).astype(BF16)
    for kind in range(3):
        advance(kind + 1, 1)
    advance(0, 3)
    for step in range(2, bits):
        for kind in range(3):
            advance(kind + 1, step)
    recv_rows(packed.at[1], back, 3)
    patch_grad[...] = mm(place, back[...]).astype(BF16)
    mine = 0
    for s in range(bits):
        mine = mine + lax.rem(me // (1 << s), 2) * (n >> (s + 1))
    proj_out[...] = term[0, mine]
    for kind in range(3):
        qkv_out[:, kind * inner:(kind + 1) * inner] = term[kind + 1, mine]
    sent_rows(packed.at[0], landed.at[0], 0)
    sent_rows(att, batt, 2)
    sent_rows(packed.at[1], back, 3)
    for c in range(4):
        for step in range(bits):
            for copy in share_copies(c, step):
                copy.wait_send()


def block(patches, send_index, window_id, norm_gain, w_qkv, w_proj, out_grad):
    n = lax.axis_size("dp")
    slots, width = patches.shape
    inner = w_proj.shape[0]
    own = width // n
    bits = n.bit_length() - 1
    vmem = pl.BlockSpec(memory_space=pltpu.VMEM)
    dma = pltpu.SemaphoreType.DMA
    embeds, patch_grad, qkv_grad, proj_grad = pl.pallas_call(
        functools.partial(block_kernel, n),
        out_shape=(
            jax.ShapeDtypeStruct((slots, width), BF16),
            jax.ShapeDtypeStruct((slots, width), BF16),
            jax.ShapeDtypeStruct((own, 3 * inner), F32),
            jax.ShapeDtypeStruct((own, inner), F32),
        ),
        in_specs=[vmem] * 7,
        out_specs=[vmem] * 4,
        scratch_shapes=[
            pltpu.VMEM((2, slots, width), BF16),
            pltpu.VMEM((2, slots, width), BF16),
            pltpu.VMEM((slots, width), BF16),
            pltpu.VMEM((slots, inner), BF16),
            pltpu.VMEM((slots, inner), BF16),
            pltpu.VMEM((slots, width), BF16),
            pltpu.VMEM((width, slots), BF16),
            pltpu.VMEM((3, HEADS, slots, HDIM), BF16),
            pltpu.VMEM((HEADS, slots, HDIM), BF16),
            pltpu.VMEM((3, slots, inner), BF16),
            pltpu.VMEM((slots, 1), F32),
            pltpu.VMEM((1, width), F32),
            pltpu.VMEM((1, slots), jnp.int32),
            pltpu.VMEM((1, slots), jnp.int32),
            pltpu.VMEM((slots, 1), jnp.int32),
            pltpu.VMEM((4, n, own, inner), F32),
            pltpu.VMEM((4, n, own, inner), jnp.int16),
            pltpu.VMEM((4, n, own, inner), jnp.int16),
            pltpu.VMEM((4, n, 1, inner), F32),
            pltpu.VMEM((4, n, 1, inner), F32),
            dma((4, n)),
            dma((4, n)),
            dma((4, bits, 2)),
            dma((4, bits, 2)),
        ],
        compiler_params=pltpu.CompilerParams(
            collective_id=0, has_side_effects=True, vmem_limit_bytes=62 * 1024 * 1024
        ),
    )(
        send_index, window_id, norm_gain, patches, out_grad, w_qkv, w_proj,
    )
    return embeds, patch_grad, qkv_grad, proj_grad.T


def solution(mesh):
    in_specs = (
        P(("groups", "dp"), None),
        P(("groups", "dp"), None, None),
        P(("groups", "dp")),
        P(),
        P(),
        P(),
        P(("groups", "dp"), None),
    )
    out_specs = (
        P(("groups", "dp"), None),
        P(("groups", "dp"), None),
        P(("groups", "dp"), None),
        P("groups", "dp"),
    )

    n = mesh.shape["dp"]

    def run(patches, send_index, *rest):
        width = patches.shape[1]
        fits = send_index.shape[2] % 16 == 0 and n & (n - 1) == 0 and width % (8 * n) == 0
        return jax.shard_map(
            block if fits else shards,
            mesh=mesh, in_specs=in_specs, out_specs=out_specs, check_vma=False,
        )(patches, send_index, *rest)

    return run
```
